32 devices in a mesh: groups: 2 (over x), row: 8 (over z, y), col: 2 (over core).
Axes of the slice: x: 2, y: 2, z: 4, core: 2. Of those that a mesh axis runs over, the one named last changes fastest.
Arguments:
- activations: bfloat16 [1536, 28672], P(('groups', 'row'), 'col'), parts along dimension 0, may hold values from -6 to 6
- gradients: bfloat16 [1536, 8192], P(('groups', 'col'), 'row'), parts along dimension 0, may hold values from -6 to 6
- input_basis: bfloat16 [28672, 14336], P('col', 'row'), may hold values from -0.03125 to 0.03125
- output_basis: bfloat16 [8192, 4096], P('row', 'col'), may hold values from -0.0625 to 0.0625
- prior_correction: float32 [8192, 14336], P(('groups', 'col'), 'row'), parts along dimension 0, may hold values from 0.5 to 2
Outputs:
- correction: float32 [8192, 14336], P(('groups', 'col'), 'row'), parts along dimension 0
The draws below stay inside these ranges and needn't reach their ends.
There are 2 independent parts, one for each index of `groups`. The reference program is written for one: setup_inputs(seed, part) draws one part's arguments, and reference() takes and returns one part's arrays. A program takes and returns all parts, laid end to end along the dimension named above; an argument that names none is the same for every part. Nothing has to cross between parts.
All inputs are finite; a program needn't handle non-finite values.
Results may differ from the reference program's by a relative error of at most 0.00036.
Values may be sent and summed in bfloat16 or wider, within the bound.
A program may use at most 256 MiB of HBM per device.

```python
import math
import jax
import jax.numpy as jnp

D_IN = 28672
D_OUT = 8192
I_WIN = 14336
O_WIN = 4096
TOKENS = 768


def steps_of(stream_key, shape, pieces, least, high):
    def one(dim, blocks):
        heights = jax.random.uniform(jax.random.fold_in(jax.random.fold_in(stream_key, 6), dim), (blocks,), jnp.float32, least / len(pieces), high / len(pieces))
        return jnp.repeat(jnp.exp(heights), shape[dim] // blocks).reshape((-1,) + (1,) * (len(shape) - dim - 1))

    factor_of = one(*pieces[0])
    for cut in pieces[1:]:
        factor_of = factor_of * one(*cut)
    return factor_of


def normal_values(key, dims, deviation, reach, shards=(), dtype=jnp.bfloat16):
    entries = jax.random.normal(key, dims, jnp.float32) * deviation
    if len(shards) > 0:
        entries = steps_of(key, dims, shards, -0.22, 0.18) * entries
    return jnp.clip(entries, min=-reach, max=reach).astype(dtype)


def setup_inputs(seed: int = 0, part: int = 0) -> dict:
    keys = jax.random.split(jax.random.key(seed), 6)
    own_keys = jax.random.split(jax.random.fold_in(keys[5], part), 6)
    activations = normal_values(own_keys[0], (TOKENS, D_IN), 1.0, 6.0, ((0, 8), (1, 2)))
    gradients = normal_values(own_keys[1], (TOKENS, D_OUT), 1.0, 6.0, ((0, 2), (1, 8)))
    input_basis = normal_values(keys[2], (D_IN, I_WIN), D_IN ** -0.5, 0.03125, ((0, 2), (1, 8)))
    output_basis = normal_values(keys[3], (D_OUT, O_WIN), D_OUT ** -0.5, 0.0625, ((0, 8), (1, 2)))
    prior_correction = jnp.clip(jnp.exp(math.log(2.0) - 1.3862944 * jax.random.uniform(own_keys[4], (O_WIN, I_WIN), jnp.float32) ** steps_of(own_keys[4], (O_WIN, I_WIN), ((0, 2), (1, 8)), -0.2, 0.2)), 0.5, 2.0)
    return dict(activations=activations, gradients=gradients, input_basis=input_basis, output_basis=output_basis, prior_correction=prior_correction)


def reference(activations, gradients, input_basis, output_basis, prior_correction):
    proj_act = jnp.dot(activations, input_basis, preferred_element_type=jnp.float32)
    sq_act = (proj_act * proj_act).astype(jnp.bfloat16)
    proj_grad = jnp.dot(gradients, output_basis, preferred_element_type=jnp.float32)
    sq_grad = (proj_grad * proj_grad).astype(jnp.bfloat16)
    increment = jnp.dot(sq_grad.T, sq_act, preferred_element_type=jnp.float32)
    return prior_correction + increment / TOKENS
```

```python
import functools

import jax
import jax.numpy as jnp
from jax import lax
from jax.experimental import pallas as pl
from jax.experimental.pallas import tpu as pltpu
from jax.sharding import PartitionSpec as P

TOKENS = 768
CHUNK = 2048
TILE = 256
RING = 8
HOPS = RING // 2


def block_of(position):
    q = lax.rem(position + 2 * RING, RING)
    return jnp.where(q < RING // 2, 2 * q, 2 * (RING - 1 - q) + 1)


def ring_kernel(
    x, g, ib, ob, sqa, sqg,
    gathered, acc, part, sums, basis, grads, rx, stage_g, stage_a,
    ag_send, ag_recv, rs_send, rs_recv, own_sem, basis_sem, g_sem, rx_send, rx_recv, sq_send, sq_recv, out_sem,
):
    rows = x.shape[0]
    chunks = x.shape[1] // CHUNK
    half = CHUNK // 2
    tokens = acc.shape[0]
    mine = tokens // 2
    tiles = acc.shape[1] // TILE

    me = lax.axis_index("row")
    core = lax.axis_index("col")
    pos = jnp.where(lax.rem(me, 2) == 0, me // 2, RING - 1 - me // 2)
    to = ({"row": block_of(pos + 1)}, {"row": block_of(pos - 1)})
    peer = {"col": 1 - core}

    def rows_of(position):
        return pl.ds(pl.multiple_of(block_of(position) * rows, 32), rows)

    barrier = pltpu.get_barrier_semaphore()
    for other in (to[0], to[1], peer):
        pl.semaphore_signal(barrier, inc=1, device_id=other, device_id_type=pl.DeviceIdType.MESH)
    pl.semaphore_wait(barrier, 3)

    order = list(range(chunks))
    order.insert(chunks - 2, None)

    def ag(i, s, d):
        chunk = order[i]
        if s == HOPS - 1:
            start, width = d * half, half
        else:
            start, width = 0, CHUNK
        where = rows_of(pos - s if d == 0 else pos + s)
        cols = pl.ds(start, width)
        dst = sqg.at[where, cols] if chunk is None else gathered.at[chunk, where, cols]
        if s > 0:
            src = dst
        elif chunk is None:
            src = stage_g
        else:
            src = x.at[:, pl.ds(chunk * CHUNK, CHUNK)]
        return pltpu.make_async_remote_copy(
            src_ref=src, dst_ref=dst, send_sem=ag_send.at[i, s, d], recv_sem=ag_recv.at[i, s, d],
            device_id=to[d], device_id_type=pl.DeviceIdType.MESH,
        )

    def send(i, s):
        for d in range(2):
            ag(i, s, d).start()

    def recv(i, s):
        for d in range(2):
            ag(i, s, d).wait_recv()

    def rs(t, d):
        src = part.at[rows_of(pos - 1 if d == 0 else pos + 1), pl.ds(d * half, half)] if t == 0 else sums.at[t - 1, d]
        return pltpu.make_async_remote_copy(
            src_ref=src, dst_ref=sums.at[t, d], send_sem=rs_send.at[t, d], recv_sem=rs_recv.at[t, d],
            device_id=to[d], device_id_type=pl.DeviceIdType.MESH,
        )

    def rs_step(t):
        for d in range(2):
            rs(t, d).wait_recv()
            own = part[rows_of(pos - 2 - t if d == 0 else pos + 2 + t), pl.ds(d * half, half)]
            total = sums[t, d] + own
            if t < RING - 2:
                sums[t, d] = total
                rs(t + 1, d).start()
            else:
                stage_g[:, pl.ds(d * half, half)] = (total * total).astype(jnp.bfloat16)
        if t == RING - 2:
            pltpu.make_async_copy(stage_g, sqg.at[rows_of(pos), :], out_sem.at[0]).start()

    def own_copy(chunk):
        return pltpu.make_async_copy(
            x.at[:, pl.ds(chunk * CHUNK, CHUNK)], gathered.at[chunk, rows_of(pos), :], own_sem.at[chunk]
        )

    def load(chunk, h):
        return pltpu.make_async_copy(ib.at[pl.ds(chunk * CHUNK + h * half, half), :], basis.at[h], basis_sem.at[h])

    def load_ob(h):
        return pltpu.make_async_copy(
            ob.at[:, pl.ds(h * half, half)], basis.at[h, :, pl.ds(0, half)], basis_sem.at[h]
        )

    def matmul(chunk):
        own_copy(chunk).wait()
        for h in range(2):
            load(chunk, h).wait()

            @pl.loop(0, tiles)
            def _(j):
                cols = pl.ds(pl.multiple_of(j * TILE, TILE), TILE)
                acc[:, cols] += jnp.dot(
                    gathered[chunk, :, pl.ds(h * half, half)], basis[h, :, cols], preferred_element_type=jnp.float32
                )

            if chunk + 1 < chunks:
                load(chunk + 1, h).start()

    send(0, 0)
    g_rows = pl.ds(pl.multiple_of(core * mine, 32), mine)
    g_remote = pltpu.make_async_remote_copy(
        src_ref=g, dst_ref=grads.at[g_rows, :], send_sem=g_sem.at[0], recv_sem=g_sem.at[1],
        device_id=peer, device_id_type=pl.DeviceIdType.MESH,
    )
    g_local = pltpu.make_async_copy(g, grads.at[g_rows, :], g_sem.at[2])
    g_remote.start()
    g_local.start()
    for h in range(2):
        load_ob(h).start()
    for chunk in range(chunks):
        own_copy(chunk).start()

    @pl.loop(0, tiles)
    def _(j):
        acc[:, pl.ds(pl.multiple_of(j * TILE, TILE), TILE)] = jnp.zeros((tokens, TILE), jnp.float32)

    g_local.wait()
    g_remote.wait()
    for h in range(2):
        load_ob(h).wait()

        @pl.loop(0, half // TILE)
        def _(j):
            cols = pl.ds(pl.multiple_of(j * TILE, TILE), TILE)
            part[:, pl.ds(pl.multiple_of(h * half + j * TILE, TILE), TILE)] = jnp.dot(
                grads[...], basis[h, :, cols], preferred_element_type=jnp.float32
            )

        load(0, h).start()
        rs(0, h).start()
    recv(0, 0)
    send(0, 1)

    last = len(order) - 1
    for i in range(last + 1):
        if i < last:
            send(i + 1, 0)
        recv(i, 1)
        send(i, 2)
        if 2 * i < RING - 1:
            rs_step(2 * i)
        if i < last:
            recv(i + 1, 0)
            send(i + 1, 1)
        recv(i, 2)
        send(i, 3)
        if 2 * i + 1 < RING - 1:
            rs_step(2 * i + 1)
        if i > 0:
            recv(i - 1, 3)
            if order[i - 1] is not None:
                matmul(order[i - 1])
    recv(last, 3)
    chunk = order[last]

    theirs = pl.ds(pl.multiple_of((1 - core) * mine, 32), mine)
    own_copy(chunk).wait()
    for h in range(2):
        load(chunk, h).wait()

    def swap(j):
        cols = pl.ds(pl.multiple_of(j * TILE, TILE), TILE)
        return pltpu.make_async_remote_copy(
            src_ref=acc.at[theirs, cols], dst_ref=rx.at[j], send_sem=rx_send.at[j], recv_sem=rx_recv.at[j],
            device_id=peer, device_id_type=pl.DeviceIdType.MESH,
        )

    def finish(j):
        cols = pl.ds(pl.multiple_of(j * TILE, TILE), TILE)
        return (
            pltpu.make_async_remote_copy(
                src_ref=stage_a.at[j], dst_ref=sqa.at[g_rows, cols], send_sem=sq_send.at[j], recv_sem=sq_recv.at[j],
                device_id=peer, device_id_type=pl.DeviceIdType.MESH,
            ),
            pltpu.make_async_copy(stage_a.at[j], sqa.at[g_rows, cols], out_sem.at[1 + j]),
        )

    @pl.loop(0, tiles)
    def _(j):
        cols = pl.ds(pl.multiple_of(j * TILE, TILE), TILE)
        total = acc[:, cols]
        for h in range(2):
            total += jnp.dot(
                gathered[chunk, :, pl.ds(h * half, half)], basis[h, :, cols], preferred_element_type=jnp.float32
            )
        acc[:, cols] = total
        swap(j).start()

    @pl.loop(0, tiles)
    def _(j):
        cols = pl.ds(pl.multiple_of(j * TILE, TILE), TILE)
        swap(j).wait_recv()
        total = acc[g_rows, cols] + rx[j]
        stage_a[j] = (total * total).astype(jnp.bfloat16)
        for copy in finish(j):
            copy.start()

    @pl.loop(0, tiles)
    def _(j):
        swap(j).wait_send()
        for copy in finish(j):
            copy.wait()

    pltpu.make_async_copy(stage_g, sqg.at[rows_of(pos), :], out_sem.at[0]).wait()
    for i in range(last + 1):
        for s in range(HOPS):
            for d in range(2):
                ag(i, s, d).wait_send()
    for t in range(RING - 1):
        for d in range(2):
            rs(t, d).wait_send()


def squares(activations, gradients, input_basis, output_basis):
    rows, width = activations.shape
    tokens = rows * RING
    columns = input_basis.shape[1]
    chunks, half, tiles = width // CHUNK, CHUNK // 2, columns // TILE
    any_spec = pl.BlockSpec(memory_space=pl.ANY)
    dma = pltpu.SemaphoreType.DMA
    return pl.pallas_call(
        ring_kernel,
        out_shape=(
            jax.ShapeDtypeStruct((tokens, columns), jnp.bfloat16),
            jax.ShapeDtypeStruct((tokens, CHUNK), jnp.bfloat16),
        ),
        in_specs=[any_spec] * 4,
        out_specs=(any_spec, any_spec),
        scratch_shapes=[
            pltpu.VMEM((chunks, tokens, CHUNK), jnp.bfloat16),
            pltpu.VMEM((tokens, columns), jnp.float32),
            pltpu.VMEM((tokens, CHUNK), jnp.float32),
            pltpu.VMEM((RING - 1, 2, rows, half), jnp.float32),
            pltpu.VMEM((2, half, columns), jnp.bfloat16),
            pltpu.VMEM((tokens, half), jnp.bfloat16),
            pltpu.VMEM((tiles, tokens // 2, TILE), jnp.float32),
            pltpu.VMEM((rows, CHUNK), jnp.bfloat16),
            pltpu.VMEM((tiles, tokens // 2, TILE), jnp.bfloat16),
            dma((chunks + 1, HOPS, 2)),
            dma((chunks + 1, HOPS, 2)),
            dma((RING - 1, 2)),
            dma((RING - 1, 2)),
            dma((chunks,)),
            dma((2,)),
            dma((3,)),
            dma((tiles,)),
            dma((tiles,)),
            dma((tiles,)),
            dma((tiles,)),
            dma((tiles + 1,)),
        ],
        compiler_params=pltpu.CompilerParams(
            collective_id=0, has_side_effects=True, vmem_limit_bytes=60 * 2**20
        ),
        cost_estimate=pl.CostEstimate(
            flops=2 * tokens * (width * columns + half * CHUNK),
            bytes_accessed=2 * (width * columns + half * CHUNK + tokens * (columns + CHUNK)),
            transcendentals=0,
        ),
    )(activations, gradients, input_basis, output_basis)


def squares_by_collectives(activations, gradients, input_basis, output_basis):
    partial_act = jnp.dot(
        lax.all_gather(activations, "row", axis=0, tiled=True),
        input_basis,
        preferred_element_type=jnp.float32,
    )
    proj_act = lax.psum(partial_act, "col")
    grad_whole = lax.all_gather(gradients, "col", axis=0, tiled=True)
    partial_grad = jnp.dot(grad_whole, output_basis, preferred_element_type=jnp.float32)
    proj_grad = lax.psum(partial_grad, "row")
    return (proj_act * proj_act).astype(jnp.bfloat16), (proj_grad * proj_grad).astype(jnp.bfloat16)


def per_device(ring, activations, gradients, input_basis, output_basis, prior_correction):
    form = squares if ring else squares_by_collectives
    sq_act, sq_grad = form(activations, gradients, input_basis, output_basis)
    increment = lax.dot_general(
        sq_grad, sq_act, (((0,), (0,)), ((), ())), preferred_element_type=jnp.float32
    )
    return prior_correction + increment / TOKENS


def solution(mesh):
    ring = mesh.shape["row"] == RING and mesh.shape["col"] == 2
    return jax.shard_map(
        functools.partial(per_device, ring),
        mesh=mesh,
        in_specs=(
            P(("groups", "row"), "col"),
            P(("groups", "col"), "row"),
            P("col", "row"),
            P("row", "col"),
            P(("groups", "col"), "row"),
        ),
        out_specs=P(("groups", "col"), "row"),
        check_vma=False,
    )
```

```python
import functools

import jax
import jax.numpy as jnp
from jax import lax
from jax.experimental import pallas as pl
from jax.experimental.pallas import tpu as pltpu
from jax.sharding import PartitionSpec as P

TOKENS = 768
CHUNK = 2048
TILE = 256
RING = 8
HOPS = RING // 2


def block_of(position):
    q = lax.rem(position + 2 * RING, RING)
    return jnp.where(q < RING // 2, 2 * q, 2 * (RING - 1 - q) + 1)


def ring_kernel(
    x, g, ib, ob, sqa, sqg,
    gathered, acc, part, sums, basis, grads, rx, stage_g, stage_a,
    ag_send, ag_recv, rs_send, rs_recv, own_sem, basis_sem, g_sem, rx_send, rx_recv, sq_send, sq_recv, out_sem,
):
    rows = x.shape[0]
    chunks = x.shape[1] // CHUNK
    half = CHUNK // 2
    tokens = acc.shape[0]
    mine = tokens // 2
    tiles = acc.shape[1] // TILE

    me = lax.axis_index("row")
    core = lax.axis_index("col")
    pos = jnp.where(lax.rem(me, 2) == 0, me // 2, RING - 1 - me // 2)
    to = ({"row": block_of(pos + 1)}, {"row": block_of(pos - 1)})
    peer = {"col": 1 - core}

    def rows_of(position):
        return pl.ds(pl.multiple_of(block_of(position) * rows, 32), rows)

    barrier = pltpu.get_barrier_semaphore()
    for other in (to[0], to[1], peer):
        pl.semaphore_signal(barrier, inc=1, device_id=other, device_id_type=pl.DeviceIdType.MESH)
    pl.semaphore_wait(barrier, 3)

    order = list(range(chunks))
    order.append(None)

    def ag(i, s, d):
        chunk = order[i]
        if s == HOPS - 1:
            start, width = d * half, half
        else:
            start, width = 0, CHUNK
        where = rows_of(pos - s if d == 0 else pos + s)
        cols = pl.ds(start, width)
        dst = sqg.at[where, cols] if chunk is None else gathered.at[chunk, where, cols]
        if s > 0:
            src = dst
        elif chunk is None:
            src = stage_g
        else:
            src = x.at[:, pl.ds(chunk * CHUNK, CHUNK)]
        return pltpu.make_async_remote_copy(
            src_ref=src, dst_ref=dst, send_sem=ag_send.at[i, s, d], recv_sem=ag_recv.at[i, s, d],
            device_id=to[d], device_id_type=pl.DeviceIdType.MESH,
        )

    def send(i, s):
        for d in range(2):
            ag(i, s, d).start()

    def recv(i, s):
        for d in range(2):
            ag(i, s, d).wait_recv()

    def rs(t, d):
        src = part.at[rows_of(pos - 1 if d == 0 else pos + 1), pl.ds(d * half, half)] if t == 0 else sums.at[t - 1, d]
        return pltpu.make_async_remote_copy(
            src_ref=src, dst_ref=sums.at[t, d], send_sem=rs_send.at[t, d], recv_sem=rs_recv.at[t, d],
            device_id=to[d], device_id_type=pl.DeviceIdType.MESH,
        )

    def rs_step(t):
        for d in range(2):
            rs(t, d).wait_recv()
            own = part[rows_of(pos - 2 - t if d == 0 else pos + 2 + t), pl.ds(d * half, half)]
            total = sums[t, d] + own
            if t < RING - 2:
                sums[t, d] = total
                rs(t + 1, d).start()
            else:
                stage_g[:, pl.ds(d * half, half)] = (total * total).astype(jnp.bfloat16)
        if t == RING - 2:
            pltpu.make_async_copy(stage_g, sqg.at[rows_of(pos), :], out_sem.at[0]).start()

    def own_copy(chunk):
        return pltpu.make_async_copy(
            x.at[:, pl.ds(chunk * CHUNK, CHUNK)], gathered.at[chunk, rows_of(pos), :], own_sem.at[chunk]
        )

    def load(chunk, h):
        return pltpu.make_async_copy(ib.at[pl.ds(chunk * CHUNK + h * half, half), :], basis.at[h], basis_sem.at[h])

    def load_ob(h):
        return pltpu.make_async_copy(
            ob.at[:, pl.ds(h * half, half)], basis.at[h, :, pl.ds(0, half)], basis_sem.at[h]
        )

    def matmul(chunk):
        own_copy(chunk).wait()
        for h in range(2):
            load(chunk, h).wait()

            @pl.loop(0, tiles)
            def _(j):
                cols = pl.ds(pl.multiple_of(j * TILE, TILE), TILE)
                acc[:, cols] += jnp.dot(
                    gathered[chunk, :, pl.ds(h * half, half)], basis[h, :, cols], preferred_element_type=jnp.float32
                )

            if chunk + 1 < chunks:
                load(chunk + 1, h).start()

    send(0, 0)
    g_rows = pl.ds(pl.multiple_of(core * mine, 32), mine)
    g_remote = pltpu.make_async_remote_copy(
        src_ref=g, dst_ref=grads.at[g_rows, :], send_sem=g_sem.at[0], recv_sem=g_sem.at[1],
        device_id=peer, device_id_type=pl.DeviceIdType.MESH,
    )
    g_local = pltpu.make_async_copy(g, grads.at[g_rows, :], g_sem.at[2])
    g_remote.start()
    g_local.start()
    for h in range(2):
        load_ob(h).start()
    for chunk in range(chunks):
        own_copy(chunk).start()

    @pl.loop(0, tiles)
    def _(j):
        acc[:, pl.ds(pl.multiple_of(j * TILE, TILE), TILE)] = jnp.zeros((tokens, TILE), jnp.float32)

    g_local.wait()
    g_remote.wait()
    for h in range(2):
        load_ob(h).wait()

        @pl.loop(0, half // TILE)
        def _(j):
            cols = pl.ds(pl.multiple_of(j * TILE, TILE), TILE)
            part[:, pl.ds(pl.multiple_of(h * half + j * TILE, TILE), TILE)] = jnp.dot(
                grads[...], basis[h, :, cols], preferred_element_type=jnp.float32
            )

        load(0, h).start()
        rs(0, h).start()
    send(1, 0)
    recv(0, 0)
    send(0, 1)

    last = len(order) - 1
    for i in range(last + 1):
        if 0 < i < last:
            send(i + 1, 0)
        recv(i, 1)
        send(i, 2)
        if 2 * i < RING - 1:
            rs_step(2 * i)
        if i < last:
            recv(i + 1, 0)
            send(i + 1, 1)
        recv(i, 2)
        send(i, 3)
        if 2 * i + 1 < RING - 1:
            rs_step(2 * i + 1)
        if i > 0:
            recv(i - 1, 3)
            if i < last:
                matmul(order[i - 1])
    chunk = order[last - 1]

    theirs = pl.ds(pl.multiple_of((1 - core) * mine, 32), mine)
    own_copy(chunk).wait()
    for h in range(2):
        load(chunk, h).wait()

    def swap(j):
        cols = pl.ds(pl.multiple_of(j * TILE, TILE), TILE)
        return pltpu.make_async_remote_copy(
            src_ref=acc.at[theirs, cols], dst_ref=rx.at[j], send_sem=rx_send.at[j], recv_sem=rx_recv.at[j],
            device_id=peer, device_id_type=pl.DeviceIdType.MESH,
        )

    def finish(j):
        cols = pl.ds(pl.multiple_of(j * TILE, TILE), TILE)
        return (
            pltpu.make_async_remote_copy(
                src_ref=stage_a.at[j], dst_ref=sqa.at[g_rows, cols], send_sem=sq_send.at[j], recv_sem=sq_recv.at[j],
                device_id=peer, device_id_type=pl.DeviceIdType.MESH,
            ),
            pltpu.make_async_copy(stage_a.at[j], sqa.at[g_rows, cols], out_sem.at[1 + j]),
        )

    @pl.loop(0, tiles)
    def _(j):
        cols = pl.ds(pl.multiple_of(j * TILE, TILE), TILE)
        total = acc[:, cols]
        for h in range(2):
            total += jnp.dot(
                gathered[chunk, :, pl.ds(h * half, half)], basis[h, :, cols], preferred_element_type=jnp.float32
            )
        acc[:, cols] = total
        swap(j).start()

    @pl.loop(0, tiles)
    def _(j):
        cols = pl.ds(pl.multiple_of(j * TILE, TILE), TILE)
        swap(j).wait_recv()
        total = acc[g_rows, cols] + rx[j]
        stage_a[j] = (total * total).astype(jnp.bfloat16)
        for copy in finish(j):
            copy.start()

    @pl.loop(0, tiles)
    def _(j):
        swap(j).wait_send()
        for copy in finish(j):
            copy.wait()

    recv(last, 3)
    pltpu.make_async_copy(stage_g, sqg.at[rows_of(pos), :], out_sem.at[0]).wait()
    for i in range(last + 1):
        for s in range(HOPS):
            for d in range(2):
                ag(i, s, d).wait_send()
    for t in range(RING - 1):
        for d in range(2):
            rs(t, d).wait_send()


def squares(activations, gradients, input_basis, output_basis):
    rows, width = activations.shape
    tokens = rows * RING
    columns = input_basis.shape[1]
    chunks, half, tiles = width // CHUNK, CHUNK // 2, columns // TILE
    any_spec = pl.BlockSpec(memory_space=pl.ANY)
    dma = pltpu.SemaphoreType.DMA
    return pl.pallas_call(
        ring_kernel,
        out_shape=(
            jax.ShapeDtypeStruct((tokens, columns), jnp.bfloat16),
            jax.ShapeDtypeStruct((tokens, CHUNK), jnp.bfloat16),
        ),
        in_specs=[any_spec] * 4,
        out_specs=(any_spec, any_spec),
        scratch_shapes=[
            pltpu.VMEM((chunks, tokens, CHUNK), jnp.bfloat16),
            pltpu.VMEM((tokens, columns), jnp.float32),
            pltpu.VMEM((tokens, CHUNK), jnp.float32),
            pltpu.VMEM((RING - 1, 2, rows, half), jnp.float32),
            pltpu.VMEM((2, half, columns), jnp.bfloat16),
            pltpu.VMEM((tokens, half), jnp.bfloat16),
            pltpu.VMEM((tiles, tokens // 2, TILE), jnp.float32),
            pltpu.VMEM((rows, CHUNK), jnp.bfloat16),
            pltpu.VMEM((tiles, tokens // 2, TILE), jnp.bfloat16),
            dma((chunks + 1, HOPS, 2)),
            dma((chunks + 1, HOPS, 2)),
            dma((RING - 1, 2)),
            dma((RING - 1, 2)),
            dma((chunks,)),
            dma((2,)),
            dma((3,)),
            dma((tiles,)),
            dma((tiles,)),
            dma((tiles,)),
            dma((tiles,)),
            dma((tiles + 1,)),
        ],
        compiler_params=pltpu.CompilerParams(
            collective_id=0, has_side_effects=True, vmem_limit_bytes=60 * 2**20
        ),
        cost_estimate=pl.CostEstimate(
            flops=2 * tokens * (width * columns + half * CHUNK),
            bytes_accessed=2 * (width * columns + half * CHUNK + tokens * (columns + CHUNK)),
            transcendentals=0,
        ),
    )(activations, gradients, input_basis, output_basis)


def squares_by_collectives(activations, gradients, input_basis, output_basis):
    partial_act = jnp.dot(
        lax.all_gather(activations, "row", axis=0, tiled=True),
        input_basis,
        preferred_element_type=jnp.float32,
    )
    proj_act = lax.psum(partial_act, "col")
    grad_whole = lax.all_gather(gradients, "col", axis=0, tiled=True)
    partial_grad = jnp.dot(grad_whole, output_basis, preferred_element_type=jnp.float32)
    proj_grad = lax.psum(partial_grad, "row")
    return (proj_act * proj_act).astype(jnp.bfloat16), (proj_grad * proj_grad).astype(jnp.bfloat16)


def per_device(ring, activations, gradients, input_basis, output_basis, prior_correction):
    form = squares if ring else squares_by_collectives
    sq_act, sq_grad = form(activations, gradients, input_basis, output_basis)
    increment = lax.dot_general(
        sq_grad, sq_act, (((0,), (0,)), ((), ())), preferred_element_type=jnp.float32
    )
    return prior_correction + increment / TOKENS


def solution(mesh):
    ring = mesh.shape["row"] == RING and mesh.shape["col"] == 2
    return jax.shard_map(
        functools.partial(per_device, ring),
        mesh=mesh,
        in_specs=(
            P(("groups", "row"), "col"),
            P(("groups", "col"), "row"),
            P("col", "row"),
            P("row", "col"),
            P(("groups", "col"), "row"),
        ),
        out_specs=P(("groups", "col"), "row"),
        check_vma=False,
    )
```
